512 devices in a mesh: ctx: 32 (over y, x), tp: 16 (over z, core).
Axes of the slice: x: 4, y: 8, z: 8, core: 2. Of those that a mesh axis runs over, the one named last changes fastest.
Arguments:
- query_lin: bfloat16 [64, 8192, 128], P('tp', 'ctx'), may hold values from -6 to 6
- key_lin: bfloat16 [64, 8192, 128], P('tp', 'ctx'), may hold values from -6 to 6
- value_lin: bfloat16 [64, 8192, 128], P('tp', 'ctx'), may hold values from -16 to 16
- decay_log: float32 [64, 8192], P('tp', 'ctx'), may hold values from -1 to 0
- norm_gain: float32 [64, 128], P('tp'), may hold values from 0.1 to 1.9
- query_soft: bfloat16 [64, 8192, 128], P('tp', 'ctx'), may hold values from -5 to 5
- key_soft: bfloat16 [64, 8192, 128], P('tp', 'ctx'), may hold values from -5 to 5
- value_soft: bfloat16 [64, 8192, 128], P('tp', 'ctx'), may hold values from -6 to 6
- doc_lengths: int32 [32], replicated, may hold values from 1 to 1024, 8192 in all
Outputs:
- lightning: bfloat16 [64, 8192, 128], P('tp', 'ctx')
- attended: bfloat16 [64, 8192, 128], P('tp', 'ctx')
The draws below stay inside these ranges and needn't reach their ends.
Inputs may be any that keep to these rules, and one draw needn't show every extreme that they name: `doc_lengths`: each document has at least one token; one has exactly 1024.
All inputs are finite; a program needn't handle non-finite values.
Results may differ from the reference program's by a relative error of at most 0.023.
Values may be sent and summed in bfloat16 or wider, within the bound.
A program may use at most 64 MiB of HBM per device.

```python
import math
import jax
import jax.numpy as jnp
import numpy as np
from jax import lax

HD = 128
HEAD_TOTAL = 64
T_DEV = 256
PACKED_LENGTH = 8192
SPAN = 4
MOST = 1024
NDOC = 32


def draw_query_soft(key, part):
    key = jax.random.fold_in(key, 11)
    return jnp.clip(jax.random.normal(key, (HEAD_TOTAL, PACKED_LENGTH, HD), jnp.float32), -5.0, 5.0).astype(jnp.bfloat16)


def draw_key_soft(key, part):
    key = jax.random.fold_in(key, 12)
    return jnp.clip(jax.random.normal(key, (HEAD_TOTAL, PACKED_LENGTH, HD), jnp.float32), -5.0, 5.0).astype(jnp.bfloat16)


def draw_value_lin(key, part):
    key = jax.random.fold_in(key, 31)
    head_share = jnp.arange(HEAD_TOTAL, dtype=jnp.float32) / max(HEAD_TOTAL - 1, 1)
    background = jnp.clip(jax.random.normal(key, (HEAD_TOTAL, PACKED_LENGTH, HD), jnp.float32), -5.0, 5.0)
    rise = jnp.exp(math.log(3.0) * head_share)
    return (background * rise[:, None, None]).astype(jnp.bfloat16)


def draw_decay_log(key, part):
    key = jax.random.fold_in(key, 21)
    random_key_brief, random_key_rapid, random_key_gradual, random_key_block, random_key_offset, random_key_location, random_key_spike = jax.random.split(key, 7)
    quick_limit = 7
    quick_heads = jax.random.randint(random_key_brief, (HEAD_TOTAL,), 0, 20) < quick_limit
    fast_rate = jnp.exp(jax.random.uniform(random_key_rapid, (HEAD_TOTAL,), jnp.float32, math.log(1.0 / 50.0), math.log(1.0 / 30.0)))
    slow_rate = jnp.exp(jax.random.uniform(random_key_gradual, (HEAD_TOTAL,), jnp.float32, math.log(0.3), math.log(1.5))) * (math.log(2.0) / PACKED_LENGTH)
    decay_step_speed = jnp.where(quick_heads, fast_rate, slow_rate)
    block_multiplier = jnp.exp(jax.random.uniform(random_key_block, (HEAD_TOTAL, PACKED_LENGTH // T_DEV), jnp.float32, math.log(0.5), math.log(2.0)))
    block_multiplier = jnp.repeat(block_multiplier, T_DEV, axis=1)
    random_offset = jax.random.uniform(random_key_offset, (HEAD_TOTAL, PACKED_LENGTH), jnp.float32, 0.5, 1.5)
    spike_locations = jax.random.randint(random_key_location, (2,), 0, PACKED_LENGTH)
    token_locations = jnp.arange(PACKED_LENGTH, dtype=jnp.int32)
    spike_mask = (token_locations == spike_locations[0]) | (token_locations == spike_locations[1])
    spike_draw = jax.random.uniform(random_key_spike, (HEAD_TOTAL,), jnp.float32, math.log(0.5), math.log(0.8))
    return -decay_step_speed[:, None] * block_multiplier * random_offset + jnp.where(spike_mask[None, :], spike_draw[:, None], 0.0)


def block_levels(rng, extent, pieces, least, high):
    factor_of, own = 1.0, jax.random.fold_in(rng, 6)
    for axis_at, parts in pieces:
        heights = jnp.exp(jax.random.uniform(jax.random.fold_in(own, axis_at), (parts,), jnp.float32, least / len(pieces), high / len(pieces)))
        factor_of = factor_of * jnp.repeat(heights, extent[axis_at] // parts).reshape([-1 if axis == axis_at else 1 for axis in range(len(extent))])
    return factor_of


def split_up(amount, total, limit, skew):
    portions = [(1 << 20) // math.isqrt(grade ** skew) + 1 for grade in range(2, amount + 1)]
    surplus, given = total - limit - (amount - 1), [1] * (amount - 1)
    while surplus > 0:
        free = [i for i in range(amount - 1) if given[i] < limit]
        pool, remaining = sum([portions[i] for i in free]), surplus
        for i in free:
            extra = min(limit - given[i], max(1, remaining * portions[i] // pool), surplus)
            given[i] = given[i] + extra
            surplus = surplus - extra
    return np.array([limit] + given)


def ragged_sizes(stream_key, count, total, bound, lean):
    if count == 2:
        one = jax.random.randint(stream_key, (), max(1, total - bound), min(bound, total - 1) + 1)
        return jnp.stack([one, total - one])
    lengths = jnp.asarray(split_up(count, total, bound, lean), jnp.int32)
    twos = (count - 1) // 2
    source_of, taker = lengths[1:1 + 2 * twos:2], lengths[2:2 + 2 * twos:2]
    slack = jnp.minimum(source_of - 1, bound - taker)
    passed = jax.random.randint(jax.random.fold_in(stream_key, 1), (twos,), 0, 1 << 20) % (slack + 1)
    lengths = lengths.at[1:1 + 2 * twos:2].set(source_of - passed).at[2:2 + 2 * twos:2].set(taker + passed)
    return lengths[jax.random.permutation(jax.random.fold_in(stream_key, 2), count)]


def noise(key, dims, spread, bound, pieces=(), kind=jnp.bfloat16):
    values = spread * jax.random.normal(key, dims, jnp.float32)
    if pieces:
        values = values * block_levels(key, dims, pieces, -0.22, 0.18)
    return jnp.clip(values, -bound, bound).astype(kind)


def setup_inputs(seed: int = 0) -> dict:
    arg_keys = jax.random.split(jax.random.key(seed), 10)
    return {
        "query_lin": noise(arg_keys[0], (HEAD_TOTAL, PACKED_LENGTH, HD), 1.0, 6.0, ((0, 16), (1, 32))),
        "key_lin": noise(arg_keys[1], (HEAD_TOTAL, PACKED_LENGTH, HD), 1.0, 6.0, ((0, 16), (1, 32))),
        "value_lin": draw_value_lin(jax.random.fold_in(arg_keys[9], 71), 0),
        "decay_log": draw_decay_log(jax.random.fold_in(arg_keys[9], 71), 0),
        "norm_gain": jnp.clip(1.0 + 0.18 * jax.random.normal(arg_keys[4], (HEAD_TOTAL, HD), jnp.float32), 0.1, 1.9),
        "query_soft": draw_query_soft(jax.random.fold_in(arg_keys[9], 71), 0),
        "key_soft": draw_key_soft(jax.random.fold_in(arg_keys[9], 71), 0),
        "value_soft": noise(arg_keys[7], (HEAD_TOTAL, PACKED_LENGTH, HD), 1.0, 6.0, ((0, 16), (1, 32))),
        "doc_lengths": ragged_sizes(arg_keys[8], NDOC, PACKED_LENGTH, MOST, 2).astype(jnp.int32),
    }


norm_eps = 1e-06

def rounded(values):
    return lax.optimization_barrier(values.astype(jnp.bfloat16)).astype(jnp.float32)

def document_of(doc_lengths, token_locations):
    doc_ends = jnp.cumsum(doc_lengths).astype(jnp.int32)
    return lax.optimization_barrier(jnp.sum((token_locations[:, None] >= doc_ends[None, :]).astype(jnp.int32), axis=1)).astype(jnp.int32)

def linear_block(queries, key_rows, values, decays, carried):
    size = decays.shape[1]
    cumulative = jnp.cumsum(decays, axis=1)
    differences = cumulative[:, :, None] - cumulative[:, None, :]
    indices = jnp.arange(size, dtype=jnp.int32)
    causal = indices[:, None] >= indices[None, :]
    factor = jnp.where(causal[None], jnp.exp(jnp.minimum(differences, 0.0)), 0.0)
    scores = jnp.einsum('hte,hse->hts', queries.astype(jnp.float32), key_rows.astype(jnp.float32))
    weights = rounded(scores * factor)
    within = jnp.einsum('hts,hse->hte', weights, values.astype(jnp.float32))
    scaled = rounded(queries.astype(jnp.float32) * jnp.exp(cumulative)[:, :, None])
    carried_term = jnp.einsum('hte,hef->htf', scaled, rounded(carried))
    block_decay = cumulative[:, -1]
    decayed = rounded(key_rows.astype(jnp.float32) * jnp.exp(block_decay[:, None] - cumulative)[:, :, None])
    update = jnp.einsum('hse,hsf->hef', decayed, values.astype(jnp.float32))
    return (within + carried_term, block_decay, update)

def attend(queries, key_rows, values, query_pos, key_pos, query_doc, key_doc):
    scores = jnp.einsum('hte,hse->hts', queries.astype(jnp.float32), key_rows.astype(jnp.float32)) * HD ** (-0.5)
    allowed = (key_pos[None, :] <= query_pos[:, None]) & (key_pos[None, :] >= 0) & (key_doc[None, :] == query_doc[:, None])
    scores = jnp.where(allowed[None], scores, -jnp.inf)
    row_max = lax.optimization_barrier(jnp.max(scores, axis=2, keepdims=True))
    weights = jnp.exp(scores - row_max)
    row_total = lax.optimization_barrier(jnp.sum(weights, axis=2, keepdims=True))
    mixed = jnp.einsum('hts,hse->hte', rounded(weights), values.astype(jnp.float32))
    return (mixed / row_total).astype(jnp.bfloat16)

def reference(query_lin, key_lin, value_lin, decay_log, norm_gain, query_soft, key_soft, value_soft, doc_lengths):
    head_count = query_lin.shape[0]
    blocks = PACKED_LENGTH // T_DEV
    query_act = jax.nn.silu(query_lin.astype(jnp.float32)).astype(jnp.bfloat16)
    key_act = jax.nn.silu(key_lin.astype(jnp.float32)).astype(jnp.bfloat16)

    def to_blocks(array):
        return jnp.moveaxis(array.reshape((head_count, blocks, T_DEV) + array.shape[2:]), 1, 0)

    def advance(carried, operands):
        queries, key_rows, values, decays = operands
        output, block_decay, update = linear_block(queries, key_rows, values, decays, carried)
        return (jnp.exp(block_decay)[:, None, None] * carried + update, output)
    initial = jnp.zeros((head_count, HD, HD), jnp.float32)
    _, outputs = lax.scan(advance, initial, (to_blocks(query_act), to_blocks(key_act), to_blocks(value_lin), to_blocks(decay_log)))
    linear_out = jnp.moveaxis(outputs, 0, 1).reshape(head_count, PACKED_LENGTH, HD)
    mean_square = lax.optimization_barrier(jnp.sum(linear_out * linear_out, axis=(0, 2))) / (head_count * HD)
    lightning = (linear_out * lax.rsqrt(mean_square + norm_eps)[None, :, None] * norm_gain[:, None, :]).astype(jnp.bfloat16)
    mixed_query = (query_soft.astype(jnp.float32) + lightning.astype(jnp.float32)).astype(jnp.bfloat16)
    lookback = SPAN * T_DEV
    window = lookback + T_DEV
    padded_keys = jnp.pad(key_soft, ((0, 0), (lookback, 0), (0, 0)))
    padded_values = jnp.pad(value_soft, ((0, 0), (lookback, 0), (0, 0)))

    def one_block(block_index):
        first_row = (block_index * T_DEV).astype(jnp.int32)
        queries = lax.dynamic_slice_in_dim(mixed_query, first_row, T_DEV, 1)
        key_rows = lax.dynamic_slice_in_dim(padded_keys, first_row, window, 1)
        values = lax.dynamic_slice_in_dim(padded_values, first_row, window, 1)
        query_pos = first_row + jnp.arange(T_DEV, dtype=jnp.int32)
        key_pos = first_row - lookback + jnp.arange(window, dtype=jnp.int32)
        query_doc = document_of(doc_lengths, query_pos)
        key_doc = document_of(doc_lengths, key_pos)
        return attend(queries, key_rows, values, query_pos, key_pos, query_doc, key_doc)
    attended = lax.map(one_block, jnp.arange(blocks, dtype=jnp.int32))
    attended = jnp.moveaxis(attended, 0, 1).reshape(head_count, PACKED_LENGTH, HD)
    return (lightning, attended)
```

```python
import functools

import jax
import jax.numpy as jnp
from jax import lax
from jax.experimental import pallas as pl
from jax.experimental.pallas import tpu as pltpu
from jax.sharding import PartitionSpec as P

MESH = pl.DeviceIdType.MESH
F32, BF16 = jnp.float32, jnp.bfloat16
NX = 4
SPAN = 4
EPS = 1e-06
FAR = -1e30
HIGH = lax.Precision.HIGHEST


def ring(step, count):
    return min(step, count - step)


def mm(a, b, dims, precision=None):
    return lax.dot_general(a, b, (dims, ((), ())), precision=precision, preferred_element_type=F32)


def silu(v):
    v = v.astype(F32)
    return (v / (1.0 + jnp.exp(-v))).astype(BF16)


def kernel(
    nctx, ntp,
    ql_h, kl_h, vl_h, dec_ref, gain_ref, qs_h, ks_h, vs_h, doc_ref,
    light_h, att_h,
    ql, kl, vl, qs, kv, kact, sq, lin, light, att, bias,
    ub, p1, sb, p2, gb, g1, psb, ps1,
    lsem, u_s, u_r, g_s, g_r, c_s, c_r, p_s, p_r,
    s4_s, s4_r, s1_s, s1_r, s3_s, s3_r, sp_s, sp_r, sm_s, sm_r, osem,
):
    heads, rows, width = ql.shape
    ny, nz = nctx // NX, ntp // 2
    c, t = lax.axis_index("ctx"), lax.axis_index("tp")
    y, x = c // NX, lax.rem(c, NX)
    per = heads * width // nctx
    per_head = width // per

    around = [(dx, dy) for dx in range(NX) for dy in range(ny) if dx or dy]
    around.sort(key=lambda o: -(ring(o[0], NX) + ring(o[1], ny)))
    stack = [(dz, dc) for dz in range(nz) for dc in range(2) if dz or dc]
    stack.sort(key=lambda o: -(2 * ring(o[0], nz) + o[1]))

    def ctx_at(dx, dy):
        return lax.rem(y + dy, ny) * NX + lax.rem(x + dx, NX)

    def tp_at(dz, dc):
        return lax.rem(t // 2 + dz, nz) * 2 + lax.rem(lax.rem(t, 2) + dc, 2)

    barrier = pltpu.get_barrier_semaphore()
    for o in around:
        pl.semaphore_signal(barrier, inc=1, device_id=(ctx_at(*o), t), device_id_type=MESH)
    for o in stack:
        pl.semaphore_signal(barrier, inc=1, device_id=(c, tp_at(*o)), device_id_type=MESH)

    loads = [
        pltpu.make_async_copy(src, dst, lsem.at[i])
        for i, (src, dst) in enumerate(
            [(kl_h, kl), (vl_h, vl), (ks_h, kv.at[0, :, 0]), (vs_h, kv.at[0, :, 1]), (ql_h, ql), (qs_h, qs)]
        )
    ]
    for load in loads:
        load.start()

    early = lax.broadcasted_iota(jnp.int32, (rows, rows), 0)
    late = lax.broadcasted_iota(jnp.int32, (rows, rows), 1)
    cum = mm(dec_ref[...], (early <= late).astype(F32), ((1,), (0,)), HIGH)
    lane_head = lax.broadcasted_iota(jnp.int32, (heads, heads * width), 1) // width
    own_head = lax.broadcasted_iota(jnp.int32, (heads, heads * width), 0)
    spread = mm(cum, (lane_head == own_head).astype(F32), ((0,), (0,)), HIGH)

    def cols(h):
        return spread[:, h * width:(h + 1) * width]

    loads[0].wait()
    loads[1].wait()
    for h in range(heads):
        ch = cols(h)
        last = ch[rows - 1:rows, :]
        gb[h] = jnp.exp(last)
        k = silu(kl[h])
        kact[h] = k
        dk = (k.astype(F32) * jnp.exp(last - ch)).astype(BF16)
        u = mm(dk, vl[h], ((0,), (0,)))
        ub[pl.ds(h * per_head, per_head)] = u.astype(BF16).reshape(per_head, per, width)
    p1[c] = ub[c]
    g1[c] = gb[c // per_head]

    pl.semaphore_wait(barrier, len(around) + len(stack))

    def g_copy(o):
        p = ctx_at(*o)
        return pltpu.make_async_remote_copy(
            src_ref=gb.at[p // per_head], dst_ref=g1.at[c], send_sem=g_s, recv_sem=g_r,
            device_id=(p, t), device_id_type=MESH)

    def u_copy(o):
        p = ctx_at(*o)
        return pltpu.make_async_remote_copy(
            src_ref=ub.at[p], dst_ref=p1.at[c], send_sem=u_s, recv_sem=u_r,
            device_id=(p, t), device_id_type=MESH)

    def c_copy(o):
        p = ctx_at(*o)
        return pltpu.make_async_remote_copy(
            src_ref=sb.at[p], dst_ref=p2.at[c], send_sem=c_s, recv_sem=c_r,
            device_id=(p, t), device_id_type=MESH)

    def p_copy(o):
        return pltpu.make_async_remote_copy(
            src_ref=psb, dst_ref=ps1.at[t], send_sem=p_s, recv_sem=p_r,
            device_id=(c, tp_at(*o)), device_id_type=MESH)

    def wait_bytes(ref, count, sem):
        part = ref.at[pl.ds(0, count)]
        pltpu.make_async_copy(part, part, sem).wait()

    def move(src, dst, h, send, recv, to):
        return pltpu.make_async_remote_copy(
            src_ref=src, dst_ref=dst, send_sem=send.at[h], recv_sem=recv.at[h],
            device_id=(to, t), device_id_type=MESH)

    def s4(h):
        return move(kv.at[0, h], kv.at[4, h], h, s4_s, s4_r, ctx_at(0, 1))

    def s1(h):
        return move(kv.at[4 * (x // (NX - 1)), h], kv.at[1, h], h, s1_s, s1_r, ctx_at(1, 0))

    def s3(h):
        return move(kv.at[4 * ((x + NX - 1) // NX), h], kv.at[3, h], h, s3_s, s3_r, ctx_at(NX - 1, 0))

    def sp(h):
        return move(kv.at[1, h, 0], kv.at[2, h, 0], h, sp_s, sp_r, lax.rem(c + 1, nctx))

    def sm(h):
        return move(kv.at[3, h, 1], kv.at[2, h, 1], h, sm_s, sm_r, lax.rem(c + nctx - 1, nctx))

    def send_own(h):
        s4(h).start()

        @pl.when(x < NX - 1)
        def _():
            s1(h).start()

        @pl.when(x == 0)
        def _():
            s3(h).start()

    def pass_on(h):
        s4(h).wait_recv()

        @pl.when(x == NX - 1)
        def _():
            s1(h).start()

        @pl.when(x > 0)
        def _():
            s3(h).start()

    def pass_second(h):
        s1(h).wait_recv()
        sp(h).start()
        s3(h).wait_recv()
        sm(h).start()

    for o in around:
        g_copy(o).start()
    for o in around:
        u_copy(o).start()
    loads[2].wait()
    loads[3].wait()
    send_own(0)

    loads[4].wait()
    for h in range(heads):
        ch = cols(h)
        q = silu(ql[h])
        sq[h] = (q.astype(F32) * jnp.exp(ch)).astype(BF16)
        gap = jnp.concatenate([ch] * (rows // width), axis=1) - cum[h:h + 1, :]
        factor = jnp.where(early >= late, jnp.exp(jnp.minimum(gap, 0.0)), 0.0)
        w = (mm(q, kact[h], ((1,), (1,))) * factor).astype(BF16)
        lin[h] = mm(w, vl[h], ((1,), (0,)))

    wait_bytes(g1, nctx - 1, g_r)
    wait_bytes(p1, nctx - 1, u_r)
    state = jnp.zeros((per, width), F32)
    for d in range(nctx):
        sb[d] = state.astype(BF16)
        if d < nctx - 1:
            state = state * g1[d] + p1[d].astype(F32)
    p2[c] = sb[c]
    for o in around:
        c_copy(o).start()
    for h in range(1, heads):
        send_own(h)
    pass_on(0)

    where_q = c * rows + lax.broadcasted_iota(jnp.int32, (rows, width), 0)
    first = jnp.zeros((rows, width), jnp.int32)
    at = jnp.int32(0)
    for d in range(doc_ref.shape[0]):
        first = jnp.where(where_q >= at, jnp.maximum(first, at), first)
        at = at + doc_ref[d]
    first = jnp.concatenate([first] * (rows // width), axis=1)
    for k in range(SPAN + 1):
        keep = (c - k) * rows + late >= first
        if k == 0:
            keep = keep & (late <= early)
        bias[k] = jnp.where(keep, 0.0, FAR)

    wait_bytes(p2, nctx - 1, c_r)
    total = jnp.zeros((rows, width), F32)
    for h in range(heads):
        carried = p2[pl.ds(h * per_head, per_head)].reshape(width, width)
        out = lin[h] + mm(sq[h], carried, ((1,), (0,)))
        lin[h] = out
        total = total + out * out
    summed = mm(jnp.ones((8, width), F32), total, ((1,), (1,)), HIGH)[0:1, :]
    psb[...] = summed
    ps1[t] = summed
    for o in stack:
        p_copy(o).start()
    for h in range(1, heads):
        pass_on(h)
    pass_second(0)

    wait_bytes(ps1, ntp - 1, p_r)
    mean = mm(ps1[:, 0, :], jnp.ones((ntp, width), F32), ((0,), (0,)), HIGH) * (1.0 / (heads * ntp * width))
    scale = lax.rsqrt(mean + EPS)
    loads[5].wait()
    for h in range(heads):
        low = (lin[h] * scale * gain_ref[h:h + 1, :]).astype(BF16)
        light[h] = low
        qs[h] = (qs[h].astype(F32) + low.astype(F32)).astype(BF16)
    out_light = pltpu.make_async_copy(light, light_h, osem.at[heads])
    out_light.start()

    factor = width ** -0.5 * 1.4426950408889634
    for h in range(heads):
        if h + 1 < heads:
            pass_second(h + 1)
        sp(h).wait_recv()
        sm(h).wait_recv()
        q = qs[h]
        parts = [mm(q, kv[k, h, 0], ((1,), (1,))) + bias[k] for k in range(SPAN + 1)]
        top = parts[0]
        for part in parts[1:]:
            top = jnp.maximum(top, part)
        top = jnp.max(top, axis=1, keepdims=True)
        amount = jnp.zeros((rows, rows), F32)
        mixed = jnp.zeros((rows, width), F32)
        for k, part in enumerate(parts):
            weights = jnp.exp2((part - top) * factor)
            amount = amount + weights
            mixed = mixed + mm(weights.astype(BF16), kv[k, h, 1], ((1,), (0,)))
        att[h] = (mixed / jnp.sum(amount, axis=1, keepdims=True)).astype(BF16)
        pltpu.make_async_copy(att.at[h], att_h.at[h], osem.at[h]).start()

    out_light.wait()
    for h in range(heads):
        pltpu.make_async_copy(att.at[h], att_h.at[h], osem.at[h]).wait()
        for copy in (s4, s1, s3, sp, sm):
            copy(h).wait_send()
    wait_bytes(g1, nctx - 1, g_s)
    wait_bytes(p1, nctx - 1, u_s)
    wait_bytes(p2, nctx - 1, c_s)
    wait_bytes(ps1, ntp - 1, p_s)


def solution(mesh):
    nctx, ntp = mesh.shape["ctx"], mesh.shape["tp"]

    def local(ql, kl, vl, dec, gain, qs, ks, vs, doc):
        heads, rows, width = ql.shape
        per = heads * width // nctx
        any_ = pl.BlockSpec(memory_space=pl.ANY)
        vmem = pl.BlockSpec(memory_space=pltpu.VMEM)
        block = (heads, rows, width)
        dma = pltpu.SemaphoreType.DMA
        return tuple(pl.pallas_call(
            functools.partial(kernel, nctx, ntp),
            out_shape=[jax.ShapeDtypeStruct(block, BF16)] * 2,
            in_specs=[any_, any_, any_, vmem, vmem, any_, any_, any_, pl.BlockSpec(memory_space=pltpu.SMEM)],
            out_specs=[any_, any_],
            scratch_shapes=[
                pltpu.VMEM(block, BF16), pltpu.VMEM(block, BF16), pltpu.VMEM(block, BF16), pltpu.VMEM(block, BF16),
                pltpu.VMEM((SPAN + 1, heads, 2, rows, width), BF16),
                pltpu.VMEM(block, BF16), pltpu.VMEM(block, BF16), pltpu.VMEM(block, F32),
                pltpu.VMEM(block, BF16), pltpu.VMEM(block, BF16),
                pltpu.VMEM((SPAN + 1, rows, rows), F32),
                pltpu.VMEM((nctx, per, width), BF16), pltpu.VMEM((nctx, per, width), BF16),
                pltpu.VMEM((nctx, per, width), BF16), pltpu.VMEM((nctx, per, width), BF16),
                pltpu.VMEM((heads, 1, width), F32), pltpu.VMEM((nctx, 1, width), F32),
                pltpu.VMEM((1, rows), F32), pltpu.VMEM((ntp, 1, rows), F32),
                dma((6,)), dma, dma, dma, dma, dma, dma, dma, dma,
            ] + [dma((heads,))] * 10 + [dma((heads + 1,))],
            compiler_params=pltpu.CompilerParams(
                collective_id=0, has_side_effects=True, vmem_limit_bytes=60 << 20),
            cost_estimate=pl.CostEstimate(flops=900_000_000, bytes_accessed=4 << 20, transcendentals=2_000_000),
        )(ql, kl, vl, dec, gain, qs, ks, vs, doc))

    wide = P("tp", "ctx", None)
    return jax.shard_map(
        local, mesh=mesh,
        in_specs=(wide, wide, wide, P("tp", "ctx"), P("tp", None), wide, wide, wide, P()),
        out_specs=(wide, wide), check_vma=False)
```

```python
import functools

import jax
import jax.numpy as jnp
from jax import lax
from jax.experimental import pallas as pl
from jax.experimental.pallas import tpu as pltpu
from jax.sharding import PartitionSpec as P

MESH = pl.DeviceIdType.MESH
F32, BF16 = jnp.float32, jnp.bfloat16
NX = 4
SPAN = 4
EPS = 1e-06
FAR = -1e30
DIRECT = ()
RIGHT = (0, 2, 4, 6)
HIGH = lax.Precision.HIGHEST


def ring(step, count):
    return min(step, count - step)


def mm(a, b, dims, precision=None):
    return lax.dot_general(a, b, (dims, ((), ())), precision=precision, preferred_element_type=F32)


def silu(v):
    v = v.astype(F32)
    return (v / (1.0 + jnp.exp(-v))).astype(BF16)


def kernel(
    nctx, ntp,
    ql_h, kl_h, vl_h, dec_ref, gain_ref, qs_h, ks_h, vs_h, doc_ref,
    light_h, att_h,
    ql, kl, vl, qs, kv, kact, sq, lin, light, att, bias,
    ub, p1, sb, p2, gb, g1, psb, ps1,
    lsem, u_s, u_r, g_s, g_r, c_s, c_r, p_s, p_r,
    s4_s, s4_r, s1_s, s1_r, s3_s, s3_r, s2_s, s2_r, osem, in_tp,
):
    heads, rows, width = ql.shape
    ny, nz = nctx // NX, ntp // 2
    c, t = lax.axis_index("ctx"), lax.axis_index("tp")
    y, x = c // NX, lax.rem(c, NX)
    per = heads * width // nctx
    per_head = width // per

    around = [(dx, dy) for dx in range(NX) for dy in range(ny) if dx or dy]
    around.sort(key=lambda o: -(ring(o[0], NX) + ring(o[1], ny)))
    stack = [(dz, dc) for dz in range(nz) for dc in range(2) if dz or dc]
    stack.sort(key=lambda o: -(2 * ring(o[0], nz) + o[1]))

    def ctx_at(dx, dy):
        return lax.rem(y + dy, ny) * NX + lax.rem(x + dx, NX)

    def tp_at(dz, dc):
        return lax.rem(t // 2 + dz, nz) * 2 + lax.rem(lax.rem(t, 2) + dc, 2)

    barrier = pltpu.get_barrier_semaphore()
    for o in around:
        pl.semaphore_signal(barrier, inc=1, device_id=(ctx_at(*o), t), device_id_type=MESH)
    for o in stack:
        @pl.when(tp_at(*o) > t)
        def _():
            pl.semaphore_signal(barrier, inc=1, device_id=(c, tp_at(*o)), device_id_type=MESH)

    loads = [
        pltpu.make_async_copy(src, dst, lsem.at[i])
        for i, (src, dst) in enumerate(
            [(kl_h, kl), (vl_h, vl), (ks_h, kv.at[0, :, 0]), (vs_h, kv.at[0, :, 1]), (ql_h, ql), (qs_h, qs)]
        )
    ]
    for load in loads:
        load.start()

    early = lax.broadcasted_iota(jnp.int32, (rows, rows), 0)
    late = lax.broadcasted_iota(jnp.int32, (rows, rows), 1)
    cum = mm(dec_ref[...], (early <= late).astype(F32), ((1,), (0,)), HIGH)
    lane_head = lax.broadcasted_iota(jnp.int32, (heads, heads * width), 1) // width
    own_head = lax.broadcasted_iota(jnp.int32, (heads, heads * width), 0)
    spread = mm(cum, (lane_head == own_head).astype(F32), ((0,), (0,)), HIGH)

    def cols(h):
        return spread[:, h * width:(h + 1) * width]

    loads[0].wait()
    loads[1].wait()
    for h in range(heads):
        ch = cols(h)
        last = ch[rows - 1:rows, :]
        gb[h] = jnp.exp(last)
        k = silu(kl[h])
        kact[h] = k
        dk = (k.astype(F32) * jnp.exp(last - ch)).astype(BF16)
        u = mm(dk, vl[h], ((0,), (0,)))
        ub[pl.ds(h * per_head, per_head)] = u.astype(BF16).reshape(per_head, per, width)
    p1[c] = ub[c]
    g1[c] = gb[c // per_head]

    pl.semaphore_wait(barrier, len(around) + t)
    for o in stack:
        @pl.when(tp_at(*o) < t)
        def _():
            pl.semaphore_signal(in_tp, inc=1, device_id=(c, tp_at(*o)), device_id_type=MESH)

    def g_copy(o):
        p = ctx_at(*o)
        return pltpu.make_async_remote_copy(
            src_ref=gb.at[p // per_head], dst_ref=g1.at[c], send_sem=g_s, recv_sem=g_r,
            device_id=(p, t), device_id_type=MESH)

    def u_copy(o):
        p = ctx_at(*o)
        return pltpu.make_async_remote_copy(
            src_ref=ub.at[p], dst_ref=p1.at[c], send_sem=u_s, recv_sem=u_r,
            device_id=(p, t), device_id_type=MESH)

    def c_copy(o):
        p = ctx_at(*o)
        return pltpu.make_async_remote_copy(
            src_ref=sb.at[p], dst_ref=p2.at[c], send_sem=c_s, recv_sem=c_r,
            device_id=(p, t), device_id_type=MESH)

    def p_copy(o):
        return pltpu.make_async_remote_copy(
            src_ref=psb, dst_ref=ps1.at[t], send_sem=p_s, recv_sem=p_r,
            device_id=(c, tp_at(*o)), device_id_type=MESH)

    def wait_bytes(ref, count, sem):
        part = ref.at[pl.ds(0, count)]
        pltpu.make_async_copy(part, part, sem).wait()

    def move(q, src, dst, send, recv, to):
        return pltpu.make_async_remote_copy(
            src_ref=kv.at[src, q // 2, q % 2], dst_ref=kv.at[dst, q // 2, q % 2],
            send_sem=send.at[q], recv_sem=recv.at[q], device_id=(to, t), device_id_type=MESH)

    def s4(q):
        return move(q, 0, 4, s4_s, s4_r, ctx_at(0, 1))

    def s1(q):
        return move(q, 4 * (x // (NX - 1)), 1, s1_s, s1_r, ctx_at(1, 0))

    def s3(q):
        return move(q, 4 * ((x + NX - 1) // NX), 3, s3_s, s3_r, ctx_at(NX - 1, 0))

    def s3d(q):
        return move(q, 0, 3, s3_s, s3_r, lax.rem(c + NX - 1, nctx))

    def s2(q):
        if q in RIGHT:
            return move(q, 1, 2, s2_s, s2_r, lax.rem(c + 1, nctx))
        return move(q, 3, 2, s2_s, s2_r, lax.rem(c + nctx - 1, nctx))

    def down(*qs):
        for q in qs:
            s4(q).start()

    def diag(*qs):
        for q in qs:
            @pl.when(x > 0)
            def _():
                s3d(q).start()

    def own(*qs):
        for q in qs:
            @pl.when(x < NX - 1)
            def _():
                s1(q).start()

            @pl.when(x == 0)
            def _():
                s3(q).start()

    def on(*qs):
        for q in qs:
            s4(q).wait_recv()

            @pl.when(x == NX - 1)
            def _():
                s1(q).start()

            if q not in DIRECT:
                @pl.when(x > 0)
                def _():
                    s3(q).start()

    def second(*qs):
        for q in qs:
            (s1 if q in RIGHT else s3)(q).wait_recv()
            s2(q).start()

    def arrived(h):
        for q in (2 * h, 2 * h + 1):
            (s3 if q in RIGHT else s1)(q).wait_recv()
            s2(q).wait_recv()

    for o in around:
        g_copy(o).start()
    for o in around:
        u_copy(o).start()
    loads[2].wait()
    loads[3].wait()
    down(0,1,2,3)
    own(0, 1, 2, 3)

    loads[4].wait()
    for h in range(heads):
        ch = cols(h)
        q = silu(ql[h])
        sq[h] = (q.astype(F32) * jnp.exp(ch)).astype(BF16)
        gap = jnp.concatenate([ch] * (rows // width), axis=1) - cum[h:h + 1, :]
        factor = jnp.where(early >= late, jnp.exp(jnp.minimum(gap, 0.0)), 0.0)
        w = (mm(q, kact[h], ((1,), (1,))) * factor).astype(BF16)
        lin[h] = mm(w, vl[h], ((1,), (0,)))

    wait_bytes(g1, nctx - 1, g_r)
    wait_bytes(p1, nctx - 1, u_r)
    state = jnp.zeros((per, width), F32)
    for d in range(nctx):
        sb[d] = state.astype(BF16)
        if d < nctx - 1:
            state = state * g1[d] + p1[d].astype(F32)
    p2[c] = sb[c]
    for o in around:
        c_copy(o).start()
    down(4, 5, 6, 7)
    own(4, 5, 6, 7)
    on(0,1,2)
    second(0, 1)

    where_q = c * rows + lax.broadcasted_iota(jnp.int32, (rows, width), 0)
    first = jnp.zeros((rows, width), jnp.int32)
    at = jnp.int32(0)
    for d in range(doc_ref.shape[0]):
        first = jnp.where(where_q >= at, jnp.maximum(first, at), first)
        at = at + doc_ref[d]
    first = jnp.concatenate([first] * (rows // width), axis=1)
    for k in range(SPAN + 1):
        keep = (c - k) * rows + late >= first
        if k == 0:
            keep = keep & (late <= early)
        bias[k] = jnp.where(keep, 0.0, FAR)

    on(3)
    second(2)
    wait_bytes(p2, nctx - 1, c_r)
    total = jnp.zeros((rows, width), F32)
    for h in range(heads):
        carried = p2[pl.ds(h * per_head, per_head)].reshape(width, width)
        out = lin[h] + mm(sq[h], carried, ((1,), (0,)))
        lin[h] = out
        total = total + out * out
    summed = mm(jnp.ones((8, width), F32), total, ((1,), (1,)), HIGH)[0:1, :]
    psb[...] = summed
    ps1[t] = summed
    @pl.when(t < ntp - 1)
    def _():
        pl.semaphore_wait(in_tp, ntp - 1 - t)

    for o in stack:
        p_copy(o).start()
    on(4)
    second(3)
    on(5)
    second(4)
    on(6)
    second(5)
    on(7)
    second(6, 7)

    wait_bytes(ps1, ntp - 1, p_r)
    mean = mm(ps1[:, 0, :], jnp.ones((ntp, width), F32), ((0,), (0,)), HIGH) * (1.0 / (heads * ntp * width))
    scale = lax.rsqrt(mean + EPS)
    loads[5].wait()
    for h in range(heads):
        low = (lin[h] * scale * gain_ref[h:h + 1, :]).astype(BF16)
        light[h] = low
        qs[h] = (qs[h].astype(F32) + low.astype(F32)).astype(BF16)
    out_light = pltpu.make_async_copy(light, light_h, osem.at[heads])
    out_light.start()

    factor = width ** -0.5 * 1.4426950408889634
    for h in range(heads):
        arrived(h)
        q = qs[h]
        parts = [mm(q, kv[k, h, 0], ((1,), (1,))) + bias[k] for k in range(SPAN + 1)]
        top = parts[0]
        for part in parts[1:]:
            top = jnp.maximum(top, part)
        top = jnp.max(top, axis=1, keepdims=True)
        amount = jnp.zeros((rows, rows), F32)
        mixed = jnp.zeros((rows, width), F32)
        for k, part in enumerate(parts):
            weights = jnp.exp2((part - top) * factor)
            amount = amount + weights
            mixed = mixed + mm(weights.astype(BF16), kv[k, h, 1], ((1,), (0,)))
        att[h] = (mixed / jnp.sum(amount, axis=1, keepdims=True)).astype(BF16)
        pltpu.make_async_copy(att.at[h], att_h.at[h], osem.at[h]).start()

    out_light.wait()
    for h in range(heads):
        pltpu.make_async_copy(att.at[h], att_h.at[h], osem.at[h]).wait()
        for q in (2 * h, 2 * h + 1):
            for copy in (s4, s1, s3, s2):
                copy(q).wait_send()
    wait_bytes(g1, nctx - 1, g_s)
    wait_bytes(p1, nctx - 1, u_s)
    wait_bytes(p2, nctx - 1, c_s)
    wait_bytes(ps1, ntp - 1, p_s)


def solution(mesh):
    nctx, ntp = mesh.shape["ctx"], mesh.shape["tp"]

    def local(ql, kl, vl, dec, gain, qs, ks, vs, doc):
        heads, rows, width = ql.shape
        per = heads * width // nctx
        any_ = pl.BlockSpec(memory_space=pl.ANY)
        vmem = pl.BlockSpec(memory_space=pltpu.VMEM)
        block = (heads, rows, width)
        dma = pltpu.SemaphoreType.DMA
        return tuple(pl.pallas_call(
            functools.partial(kernel, nctx, ntp),
            out_shape=[jax.ShapeDtypeStruct(block, BF16)] * 2,
            in_specs=[any_, any_, any_, vmem, vmem, any_, any_, any_, pl.BlockSpec(memory_space=pltpu.SMEM)],
            out_specs=[any_, any_],
            scratch_shapes=[
                pltpu.VMEM(block, BF16), pltpu.VMEM(block, BF16), pltpu.VMEM(block, BF16), pltpu.VMEM(block, BF16),
                pltpu.VMEM((SPAN + 1, heads, 2, rows, width), BF16),
                pltpu.VMEM(block, BF16), pltpu.VMEM(block, BF16), pltpu.VMEM(block, F32),
                pltpu.VMEM(block, BF16), pltpu.VMEM(block, BF16),
                pltpu.VMEM((SPAN + 1, rows, rows), F32),
                pltpu.VMEM((nctx, per, width), BF16), pltpu.VMEM((nctx, per, width), BF16),
                pltpu.VMEM((nctx, per, width), BF16), pltpu.VMEM((nctx, per, width), BF16),
                pltpu.VMEM((heads, 1, width), F32), pltpu.VMEM((nctx, 1, width), F32),
                pltpu.VMEM((1, rows), F32), pltpu.VMEM((ntp, 1, rows), F32),
                dma((6,)), dma, dma, dma, dma, dma, dma, dma, dma,
            ] + [dma((2 * heads,))] * 8 + [dma((heads + 1,)), pltpu.SemaphoreType.REGULAR],
            compiler_params=pltpu.CompilerParams(
                collective_id=0, has_side_effects=True, vmem_limit_bytes=60 << 20),
            cost_estimate=pl.CostEstimate(flops=900_000_000, bytes_accessed=4 << 20, transcendentals=2_000_000),
        )(ql, kl, vl, dec, gain, qs, ks, vs, doc))

    wide = P("tp", "ctx", None)
    return jax.shard_map(
        local, mesh=mesh,
        in_specs=(wide, wide, wide, P("tp", "ctx"), P("tp", None), wide, wide, wide, P()),
        out_specs=(wide, wide), check_vma=False)
```

```python
import functools

import jax
import jax.numpy as jnp
from jax import lax
from jax.experimental import pallas as pl
from jax.experimental.pallas import tpu as pltpu
from jax.sharding import PartitionSpec as P

MESH = pl.DeviceIdType.MESH
F32, BF16 = jnp.float32, jnp.bfloat16
NX = 4
SPAN = 4
EPS = 1e-06
FAR = -1e30
DIRECT = ()
RIGHT = (0, 2, 4, 6)
HIGH = lax.Precision.HIGHEST


def ring(step, count):
    return min(step, count - step)


def mm(a, b, dims, precision=None):
    return lax.dot_general(a, b, (dims, ((), ())), precision=precision, preferred_element_type=F32)


def silu(v):
    v = v.astype(F32)
    return (v / (1.0 + jnp.exp(-v))).astype(BF16)


def kernel(
    nctx, ntp,
    ql_h, kl_h, vl_h, dec_ref, gain_ref, qs_h, ks_h, vs_h, doc_ref,
    out_h,
    ql, kl, vl, qs, kv, kact, sq, lin, light, att, bias,
    ub, p1, sb, p2, gb, g1, psb, ps1,
    lsem, u_s, u_r, g_s, g_r, c_s, c_r, p_s, p_r,
    s4_s, s4_r, s1_s, s1_r, s3_s, s3_r, s2_s, s2_r, osem, in_tp,
):
    heads, rows, width = ql.shape
    ny, nz = nctx // NX, ntp // 2
    c, t = lax.axis_index("ctx"), lax.axis_index("tp")
    y, x = c // NX, lax.rem(c, NX)
    per = heads * width // nctx
    per_head = width // per

    around = [(dx, dy) for dx in range(NX) for dy in range(ny) if dx or dy]
    around.sort(key=lambda o: -(ring(o[0], NX) + ring(o[1], ny)))
    stack = [(dz, dc) for dz in range(nz) for dc in range(2) if dz or dc]
    stack.sort(key=lambda o: -(2 * ring(o[0], nz) + o[1]))

    def ctx_at(dx, dy):
        return lax.rem(y + dy, ny) * NX + lax.rem(x + dx, NX)

    def tp_at(dz, dc):
        return lax.rem(t // 2 + dz, nz) * 2 + lax.rem(lax.rem(t, 2) + dc, 2)

    barrier = pltpu.get_barrier_semaphore()
    for o in around:
        pl.semaphore_signal(barrier, inc=1, device_id=(ctx_at(*o), t), device_id_type=MESH)
    for o in stack:
        @pl.when(tp_at(*o) > t)
        def _():
            pl.semaphore_signal(barrier, inc=1, device_id=(c, tp_at(*o)), device_id_type=MESH)

    loads = [
        pltpu.make_async_copy(src, dst, lsem.at[i])
        for i, (src, dst) in enumerate(
            [(kl_h, kl), (vl_h, vl), (ks_h, kv.at[0, :, 0]), (vs_h, kv.at[0, :, 1]), (ql_h, ql), (qs_h, qs)]
        )
    ]
    for load in loads:
        load.start()

    early = lax.broadcasted_iota(jnp.int32, (rows, rows), 0)
    late = lax.broadcasted_iota(jnp.int32, (rows, rows), 1)
    cum = mm(dec_ref[...], (early <= late).astype(F32), ((1,), (0,)), HIGH)
    lane_head = lax.broadcasted_iota(jnp.int32, (heads, heads * width), 1) // width
    own_head = lax.broadcasted_iota(jnp.int32, (heads, heads * width), 0)
    spread = mm(cum, (lane_head == own_head).astype(F32), ((0,), (0,)), HIGH)

    def cols(h):
        return spread[:, h * width:(h + 1) * width]

    loads[0].wait()
    loads[1].wait()
    for h in range(heads):
        ch = cols(h)
        last = ch[rows - 1:rows, :]
        gb[h] = jnp.exp(last)
        k = silu(kl[h])
        kact[h] = k
        dk = (k.astype(F32) * jnp.exp(last - ch)).astype(BF16)
        u = mm(dk, vl[h], ((0,), (0,)))
        ub[pl.ds(h * per_head, per_head)] = u.astype(BF16).reshape(per_head, per, width)
    p1[c] = ub[c]
    g1[c] = gb[c // per_head]

    pl.semaphore_wait(barrier, len(around) + t)
    for o in stack:
        @pl.when(tp_at(*o) < t)
        def _():
            pl.semaphore_signal(in_tp, inc=1, device_id=(c, tp_at(*o)), device_id_type=MESH)

    def g_copy(o):
        p = ctx_at(*o)
        return pltpu.make_async_remote_copy(
            src_ref=gb.at[p // per_head], dst_ref=g1.at[c], send_sem=g_s, recv_sem=g_r,
            device_id=(p, t), device_id_type=MESH)

    def u_copy(o):
        p = ctx_at(*o)
        return pltpu.make_async_remote_copy(
            src_ref=ub.at[p], dst_ref=p1.at[c], send_sem=u_s, recv_sem=u_r,
            device_id=(p, t), device_id_type=MESH)

    def c_copy(o):
        p = ctx_at(*o)
        return pltpu.make_async_remote_copy(
            src_ref=sb.at[p], dst_ref=p2.at[c], send_sem=c_s, recv_sem=c_r,
            device_id=(p, t), device_id_type=MESH)

    def p_copy(o):
        return pltpu.make_async_remote_copy(
            src_ref=psb, dst_ref=ps1.at[t], send_sem=p_s, recv_sem=p_r,
            device_id=(c, tp_at(*o)), device_id_type=MESH)

    def wait_bytes(ref, count, sem):
        part = ref.at[pl.ds(0, count)]
        pltpu.make_async_copy(part, part, sem).wait()

    def move(q, src, dst, send, recv, to):
        return pltpu.make_async_remote_copy(
            src_ref=kv.at[src, q // 2, q % 2], dst_ref=kv.at[dst, q // 2, q % 2],
            send_sem=send.at[q], recv_sem=recv.at[q], device_id=(to, t), device_id_type=MESH)

    def s4(q):
        return move(q, 0, 4, s4_s, s4_r, ctx_at(0, 1))

    def s1(q):
        return move(q, 4 * (x // (NX - 1)), 1, s1_s, s1_r, ctx_at(1, 0))

    def s3(q):
        return move(q, 4 * ((x + NX - 1) // NX), 3, s3_s, s3_r, ctx_at(NX - 1, 0))

    def s3d(q):
        return move(q, 0, 3, s3_s, s3_r, lax.rem(c + NX - 1, nctx))

    def s2(q):
        if q in RIGHT:
            return move(q, 1, 2, s2_s, s2_r, lax.rem(c + 1, nctx))
        return move(q, 3, 2, s2_s, s2_r, lax.rem(c + nctx - 1, nctx))

    def down(*qs):
        for q in qs:
            s4(q).start()

    def diag(*qs):
        for q in qs:
            @pl.when(x > 0)
            def _():
                s3d(q).start()

    def own(*qs):
        for q in qs:
            @pl.when(x < NX - 1)
            def _():
                s1(q).start()

            @pl.when(x == 0)
            def _():
                s3(q).start()

    def on(*qs):
        for q in qs:
            s4(q).wait_recv()

            @pl.when(x == NX - 1)
            def _():
                s1(q).start()

            if q not in DIRECT:
                @pl.when(x > 0)
                def _():
                    s3(q).start()

    def second(*qs):
        for q in qs:
            (s1 if q in RIGHT else s3)(q).wait_recv()
            s2(q).start()

    def arrived(h):
        for q in (2 * h, 2 * h + 1):
            (s3 if q in RIGHT else s1)(q).wait_recv()
            s2(q).wait_recv()

    for o in around:
        g_copy(o).start()
    for o in around:
        u_copy(o).start()
    loads[2].wait()
    loads[3].wait()
    down(0,1,2,3)
    own(0, 1, 2, 3)

    loads[4].wait()
    for h in range(heads):
        ch = cols(h)
        q = silu(ql[h])
        sq[h] = (q.astype(F32) * jnp.exp(ch)).astype(BF16)
        gap = jnp.concatenate([ch] * (rows // width), axis=1) - cum[h:h + 1, :]
        factor = jnp.where(early >= late, jnp.exp(jnp.minimum(gap, 0.0)), 0.0)
        w = (mm(q, kact[h], ((1,), (1,))) * factor).astype(BF16)
        lin[h] = mm(w, vl[h], ((1,), (0,)))

    wait_bytes(g1, nctx - 1, g_r)
    wait_bytes(p1, nctx - 1, u_r)
    state = jnp.zeros((per, width), F32)
    for d in range(nctx):
        sb[d] = state.astype(BF16)
        if d < nctx - 1:
            state = state * g1[d] + p1[d].astype(F32)
    p2[c] = sb[c]
    for o in around:
        c_copy(o).start()
    down(4, 5, 6, 7)
    own(4, 5, 6, 7)
    on(0,1,2)
    second(0, 1)

    where_q = c * rows + lax.broadcasted_iota(jnp.int32, (rows, width), 0)
    first = jnp.zeros((rows, width), jnp.int32)
    at = jnp.int32(0)
    for d in range(doc_ref.shape[0]):
        first = jnp.where(where_q >= at, jnp.maximum(first, at), first)
        at = at + doc_ref[d]
    first = jnp.concatenate([first] * (rows // width), axis=1)
    for k in range(SPAN + 1):
        keep = (c - k) * rows + late >= first
        if k == 0:
            keep = keep & (late <= early)
        bias[k] = jnp.where(keep, 0.0, FAR)

    on(3)
    second(2)
    wait_bytes(p2, nctx - 1, c_r)
    total = jnp.zeros((rows, width), F32)
    for h in range(heads):
        carried = p2[pl.ds(h * per_head, per_head)].reshape(width, width)
        out = lin[h] + mm(sq[h], carried, ((1,), (0,)))
        lin[h] = out
        total = total + out * out
    summed = mm(jnp.ones((8, width), F32), total, ((1,), (1,)), HIGH)[0:1, :]
    psb[...] = summed
    ps1[t] = summed
    @pl.when(t < ntp - 1)
    def _():
        pl.semaphore_wait(in_tp, ntp - 1 - t)

    for o in stack:
        p_copy(o).start()
    on(4)
    second(3)
    on(5)
    second(4)
    on(6)
    second(5)
    on(7)
    second(6, 7)

    wait_bytes(ps1, ntp - 1, p_r)
    mean = mm(ps1[:, 0, :], jnp.ones((ntp, width), F32), ((0,), (0,)), HIGH) * (1.0 / (heads * ntp * width))
    scale = lax.rsqrt(mean + EPS)
    loads[5].wait()
    for h in range(heads):
        low = (lin[h] * scale * gain_ref[h:h + 1, :]).astype(BF16)
        light[h] = low
        qs[h] = (qs[h].astype(F32) + low.astype(F32)).astype(BF16)
    out_light = pltpu.make_async_copy(light, out_h.at[0], osem.at[heads])
    out_light.start()

    factor = width ** -0.5 * 1.4426950408889634
    for h in range(heads):
        arrived(h)
        q = qs[h]
        parts = [mm(q, kv[k, h, 0], ((1,), (1,))) + bias[k] for k in range(SPAN + 1)]
        top = parts[0]
        for part in parts[1:]:
            top = jnp.maximum(top, part)
        top = jnp.max(top, axis=1, keepdims=True)
        amount = jnp.zeros((rows, rows), F32)
        mixed = jnp.zeros((rows, width), F32)
        for k, part in enumerate(parts):
            weights = jnp.exp2((part - top) * factor)
            amount = amount + weights
            mixed = mixed + mm(weights.astype(BF16), kv[k, h, 1], ((1,), (0,)))
        att[h] = (mixed / jnp.sum(amount, axis=1, keepdims=True)).astype(BF16)
        pltpu.make_async_copy(att.at[h], out_h.at[1, h], osem.at[h]).start()

    out_light.wait()
    for h in range(heads):
        pltpu.make_async_copy(att.at[h], out_h.at[1, h], osem.at[h]).wait()
        for q in (2 * h, 2 * h + 1):
            for copy in (s4, s1, s3, s2):
                copy(q).wait_send()
    wait_bytes(g1, nctx - 1, g_s)
    wait_bytes(p1, nctx - 1, u_s)
    wait_bytes(p2, nctx - 1, c_s)
    wait_bytes(ps1, ntp - 1, p_s)


def solution(mesh):
    nctx, ntp = mesh.shape["ctx"], mesh.shape["tp"]

    def local(ql, kl, vl, dec, gain, qs, ks, vs, doc):
        heads, rows, width = ql.shape
        per = heads * width // nctx
        any_ = pl.BlockSpec(memory_space=pl.ANY)
        vmem = pl.BlockSpec(memory_space=pltpu.VMEM)
        block = (heads, rows, width)
        dma = pltpu.SemaphoreType.DMA
        both = pl.pallas_call(
            functools.partial(kernel, nctx, ntp),
            out_shape=jax.ShapeDtypeStruct((2,) + block, BF16),
            in_specs=[any_, any_, any_, vmem, vmem, any_, any_, any_, pl.BlockSpec(memory_space=pltpu.SMEM)],
            out_specs=any_,
            scratch_shapes=[
                pltpu.VMEM(block, BF16), pltpu.VMEM(block, BF16), pltpu.VMEM(block, BF16), pltpu.VMEM(block, BF16),
                pltpu.VMEM((SPAN + 1, heads, 2, rows, width), BF16),
                pltpu.VMEM(block, BF16), pltpu.VMEM(block, BF16), pltpu.VMEM(block, F32),
                pltpu.VMEM(block, BF16), pltpu.VMEM(block, BF16),
                pltpu.VMEM((SPAN + 1, rows, rows), F32),
                pltpu.VMEM((nctx, per, width), BF16), pltpu.VMEM((nctx, per, width), BF16),
                pltpu.VMEM((nctx, per, width), BF16), pltpu.VMEM((nctx, per, width), BF16),
                pltpu.VMEM((heads, 1, width), F32), pltpu.VMEM((nctx, 1, width), F32),
                pltpu.VMEM((1, rows), F32), pltpu.VMEM((ntp, 1, rows), F32),
                dma((6,)), dma, dma, dma, dma, dma, dma, dma, dma,
            ] + [dma((2 * heads,))] * 8 + [dma((heads + 1,)), pltpu.SemaphoreType.REGULAR],
            compiler_params=pltpu.CompilerParams(
                collective_id=0, has_side_effects=True, vmem_limit_bytes=60 << 20),
            cost_estimate=pl.CostEstimate(flops=900_000_000, bytes_accessed=4 << 20, transcendentals=2_000_000),
        )(ql, kl, vl, dec, gain, qs, ks, vs, doc)
        return both[0], both[1]

    wide = P("tp", "ctx", None)
    return jax.shard_map(
        local, mesh=mesh,
        in_specs=(wide, wide, wide, P("tp", "ctx"), P("tp", None), wide, wide, wide, P()),
        out_specs=(wide, wide), check_vma=False)
```

```python
import functools

import jax
import jax.numpy as jnp
from jax import lax
from jax.experimental import pallas as pl
from jax.experimental.pallas import tpu as pltpu
from jax.sharding import PartitionSpec as P

MESH = pl.DeviceIdType.MESH
F32, BF16 = jnp.float32, jnp.bfloat16
NX = 4
SPAN = 4
EPS = 1e-06
FAR = -1e30
DIRECT = ()
RIGHT = (2, 4, 6, 7)
HIGH = lax.Precision.HIGHEST


def ring(step, count):
    return min(step, count - step)


def mm(a, b, dims, precision=None):
    return lax.dot_general(a, b, (dims, ((), ())), precision=precision, preferred_element_type=F32)


def silu(v):
    v = v.astype(F32)
    return (v / (1.0 + jnp.exp(-v))).astype(BF16)


def kernel(
    nctx, ntp,
    ql_h, kl_h, vl_h, dec_ref, gain_ref, qs_h, ks_h, vs_h, doc_ref,
    out_h,
    ql, kl, vl, qs, kv, kact, sq, lin, light, att, bias,
    ub, p1, sb, p2, gb, g1, psb, ps1,
    lsem, u_s, u_r, g_s, g_r, c_s, c_r, p_s, p_r,
    s4_s, s4_r, s1_s, s1_r, s3_s, s3_r, s2_s, s2_r, osem, in_tp,
):
    heads, rows, width = ql.shape
    ny, nz = nctx // NX, ntp // 2
    c, t = lax.axis_index("ctx"), lax.axis_index("tp")
    y, x = c // NX, lax.rem(c, NX)
    per = heads * width // nctx
    per_head = width // per

    around = [(dx, dy) for dx in range(NX) for dy in range(ny) if dx or dy]
    around.sort(key=lambda o: -(ring(o[0], NX) + ring(o[1], ny)))
    stack = [(dz, dc) for dz in range(nz) for dc in range(2) if dz or dc]
    stack.sort(key=lambda o: -(2 * ring(o[0], nz) + o[1]))

    def ctx_at(dx, dy):
        return lax.rem(y + dy, ny) * NX + lax.rem(x + dx, NX)

    def tp_at(dz, dc):
        return lax.rem(t // 2 + dz, nz) * 2 + lax.rem(lax.rem(t, 2) + dc, 2)

    barrier = pltpu.get_barrier_semaphore()
    for o in around:
        pl.semaphore_signal(barrier, inc=1, device_id=(ctx_at(*o), t), device_id_type=MESH)
    for o in stack:
        @pl.when(tp_at(*o) > t)
        def _():
            pl.semaphore_signal(barrier, inc=1, device_id=(c, tp_at(*o)), device_id_type=MESH)

    loads = [
        pltpu.make_async_copy(src, dst, lsem.at[i])
        for i, (src, dst) in enumerate(
            [(kl_h, kl), (vl_h, vl), (ks_h, kv.at[0, :, 0]), (vs_h, kv.at[0, :, 1]), (ql_h, ql), (qs_h, qs)]
        )
    ]
    for load in loads:
        load.start()

    early = lax.broadcasted_iota(jnp.int32, (rows, rows), 0)
    late = lax.broadcasted_iota(jnp.int32, (rows, rows), 1)
    cum = mm(dec_ref[...], (early <= late).astype(F32), ((1,), (0,)), HIGH)
    lane_head = lax.broadcasted_iota(jnp.int32, (heads, heads * width), 1) // width
    own_head = lax.broadcasted_iota(jnp.int32, (heads, heads * width), 0)
    spread = mm(cum, (lane_head == own_head).astype(F32), ((0,), (0,)), HIGH)

    def cols(h):
        return spread[:, h * width:(h + 1) * width]

    loads[0].wait()
    loads[1].wait()
    for h in range(heads):
        ch = cols(h)
        last = ch[rows - 1:rows, :]
        gb[h] = jnp.exp(last)
        k = silu(kl[h])
        kact[h] = k
        dk = (k.astype(F32) * jnp.exp(last - ch)).astype(BF16)
        u = mm(dk, vl[h], ((0,), (0,)))
        ub[pl.ds(h * per_head, per_head)] = u.astype(BF16).reshape(per_head, per, width)
    p1[c] = ub[c]
    g1[c] = gb[c // per_head]

    pl.semaphore_wait(barrier, len(around) + t)
    for o in stack:
        @pl.when(tp_at(*o) < t)
        def _():
            pl.semaphore_signal(in_tp, inc=1, device_id=(c, tp_at(*o)), device_id_type=MESH)

    def g_copy(o):
        p = ctx_at(*o)
        return pltpu.make_async_remote_copy(
            src_ref=gb.at[p // per_head], dst_ref=g1.at[c], send_sem=g_s, recv_sem=g_r,
            device_id=(p, t), device_id_type=MESH)

    def u_copy(o):
        p = ctx_at(*o)
        return pltpu.make_async_remote_copy(
            src_ref=ub.at[p], dst_ref=p1.at[c], send_sem=u_s, recv_sem=u_r,
            device_id=(p, t), device_id_type=MESH)

    def c_copy(o):
        p = ctx_at(*o)
        return pltpu.make_async_remote_copy(
            src_ref=sb.at[p], dst_ref=p2.at[c], send_sem=c_s, recv_sem=c_r,
            device_id=(p, t), device_id_type=MESH)

    def p_copy(o):
        return pltpu.make_async_remote_copy(
            src_ref=psb, dst_ref=ps1.at[t], send_sem=p_s, recv_sem=p_r,
            device_id=(c, tp_at(*o)), device_id_type=MESH)

    def wait_bytes(ref, count, sem):
        part = ref.at[pl.ds(0, count)]
        pltpu.make_async_copy(part, part, sem).wait()

    def move(q, src, dst, send, recv, to):
        return pltpu.make_async_remote_copy(
            src_ref=kv.at[src, q // 2, q % 2], dst_ref=kv.at[dst, q // 2, q % 2],
            send_sem=send.at[q], recv_sem=recv.at[q], device_id=(to, t), device_id_type=MESH)

    def s4(q):
        return move(q, 0, 4, s4_s, s4_r, ctx_at(0, 1))

    def s1(q):
        return move(q, 4 * (x // (NX - 1)), 1, s1_s, s1_r, ctx_at(1, 0))

    def s3(q):
        return move(q, 4 * ((x + NX - 1) // NX), 3, s3_s, s3_r, ctx_at(NX - 1, 0))

    def s3d(q):
        return move(q, 0, 3, s3_s, s3_r, lax.rem(c + NX - 1, nctx))

    def s2(q):
        if q in RIGHT:
            return move(q, 1, 2, s2_s, s2_r, lax.rem(c + 1, nctx))
        return move(q, 3, 2, s2_s, s2_r, lax.rem(c + nctx - 1, nctx))

    def down(*qs):
        for q in qs:
            s4(q).start()

    def diag(*qs):
        for q in qs:
            @pl.when(x > 0)
            def _():
                s3d(q).start()

    def own(*qs):
        for q in qs:
            @pl.when(x < NX - 1)
            def _():
                s1(q).start()

            @pl.when(x == 0)
            def _():
                s3(q).start()

    def on(*qs):
        for q in qs:
            s4(q).wait_recv()

            @pl.when(x == NX - 1)
            def _():
                s1(q).start()

            if q not in DIRECT:
                @pl.when(x > 0)
                def _():
                    s3(q).start()

    def second(*qs):
        for q in qs:
            (s1 if q in RIGHT else s3)(q).wait_recv()
            s2(q).start()

    def arrived(h):
        for q in (2 * h, 2 * h + 1):
            (s3 if q in RIGHT else s1)(q).wait_recv()
            s2(q).wait_recv()

    for o in around:
        g_copy(o).start()
    for o in around:
        u_copy(o).start()
    loads[2].wait()
    loads[3].wait()
    down(0,1,2,3)
    own(0, 1, 2, 3)

    loads[4].wait()
    for h in range(heads):
        ch = cols(h)
        q = silu(ql[h])
        sq[h] = (q.astype(F32) * jnp.exp(ch)).astype(BF16)
        gap = jnp.concatenate([ch] * (rows // width), axis=1) - cum[h:h + 1, :]
        factor = jnp.where(early >= late, jnp.exp(jnp.minimum(gap, 0.0)), 0.0)
        w = (mm(q, kact[h], ((1,), (1,))) * factor).astype(BF16)
        lin[h] = mm(w, vl[h], ((1,), (0,)))

    on(0)
    wait_bytes(g1, nctx - 1, g_r)
    wait_bytes(p1, nctx - 1, u_r)
    state = jnp.zeros((per, width), F32)
    for d in range(nctx):
        sb[d] = state.astype(BF16)
        if d < nctx - 1:
            state = state * g1[d] + p1[d].astype(F32)
    p2[c] = sb[c]
    for o in around:
        c_copy(o).start()
    down(4, 5, 6, 7)
    own(4, 5, 6, 7)
    on(1)
    second(0)
    on(2)
    second(1)

    where_q = c * rows + lax.broadcasted_iota(jnp.int32, (rows, width), 0)
    first = jnp.zeros((rows, width), jnp.int32)
    at = jnp.int32(0)
    for d in range(doc_ref.shape[0]):
        first = jnp.where(where_q >= at, jnp.maximum(first, at), first)
        at = at + doc_ref[d]
    first = jnp.concatenate([first] * (rows // width), axis=1)
    for k in range(SPAN + 1):
        keep = (c - k) * rows + late >= first
        if k == 0:
            keep = keep & (late <= early)
        bias[k] = jnp.where(keep, 0.0, FAR)

    on(3)
    second(2)
    wait_bytes(p2, nctx - 1, c_r)
    total = jnp.zeros((rows, width), F32)
    for h in range(heads):
        carried = p2[pl.ds(h * per_head, per_head)].reshape(width, width)
        out = lin[h] + mm(sq[h], carried, ((1,), (0,)))
        lin[h] = out
        total = total + out * out
    summed = mm(jnp.ones((8, width), F32), total, ((1,), (1,)), HIGH)[0:1, :]
    psb[...] = summed
    ps1[t] = summed
    @pl.when(t < ntp - 1)
    def _():
        pl.semaphore_wait(in_tp, ntp - 1 - t)

    for o in stack:
        p_copy(o).start()
    on(4)
    second(3)
    on(5)
    second(4)
    on(6)
    second(5)
    on(7)
    second(6, 7)

    wait_bytes(ps1, ntp - 1, p_r)
    mean = mm(ps1[:, 0, :], jnp.ones((ntp, width), F32), ((0,), (0,)), HIGH) * (1.0 / (heads * ntp * width))
    scale = lax.rsqrt(mean + EPS)
    loads[5].wait()
    for h in range(heads):
        low = (lin[h] * scale * gain_ref[h:h + 1, :]).astype(BF16)
        light[h] = low
        qs[h] = (qs[h].astype(F32) + low.astype(F32)).astype(BF16)
    out_light = pltpu.make_async_copy(light, out_h.at[0], osem.at[heads])
    out_light.start()

    factor = width ** -0.5 * 1.4426950408889634
    for h in range(heads):
        arrived(h)
        q = qs[h]
        parts = [mm(q, kv[k, h, 0], ((1,), (1,))) + bias[k] for k in range(SPAN + 1)]
        top = parts[0]
        for part in parts[1:]:
            top = jnp.maximum(top, part)
        top = jnp.max(top, axis=1, keepdims=True)
        amount = jnp.zeros((rows, rows), F32)
        mixed = jnp.zeros((rows, width), F32)
        for k, part in enumerate(parts):
            weights = jnp.exp2((part - top) * factor)
            amount = amount + weights
            mixed = mixed + mm(weights.astype(BF16), kv[k, h, 1], ((1,), (0,)))
        att[h] = (mixed / jnp.sum(amount, axis=1, keepdims=True)).astype(BF16)
        pltpu.make_async_copy(att.at[h], out_h.at[1, h], osem.at[h]).start()

    out_light.wait()
    for h in range(heads):
        pltpu.make_async_copy(att.at[h], out_h.at[1, h], osem.at[h]).wait()
        for q in (2 * h, 2 * h + 1):
            for copy in (s4, s1, s3, s2):
                copy(q).wait_send()
    wait_bytes(g1, nctx - 1, g_s)
    wait_bytes(p1, nctx - 1, u_s)
    wait_bytes(p2, nctx - 1, c_s)
    wait_bytes(ps1, ntp - 1, p_s)


def solution(mesh):
    nctx, ntp = mesh.shape["ctx"], mesh.shape["tp"]

    def local(ql, kl, vl, dec, gain, qs, ks, vs, doc):
        heads, rows, width = ql.shape
        per = heads * width // nctx
        any_ = pl.BlockSpec(memory_space=pl.ANY)
        vmem = pl.BlockSpec(memory_space=pltpu.VMEM)
        block = (heads, rows, width)
        dma = pltpu.SemaphoreType.DMA
        both = pl.pallas_call(
            functools.partial(kernel, nctx, ntp),
            out_shape=jax.ShapeDtypeStruct((2,) + block, BF16),
            in_specs=[any_, any_, any_, vmem, vmem, any_, any_, any_, pl.BlockSpec(memory_space=pltpu.SMEM)],
            out_specs=any_,
            scratch_shapes=[
                pltpu.VMEM(block, BF16), pltpu.VMEM(block, BF16), pltpu.VMEM(block, BF16), pltpu.VMEM(block, BF16),
                pltpu.VMEM((SPAN + 1, heads, 2, rows, width), BF16),
                pltpu.VMEM(block, BF16), pltpu.VMEM(block, BF16), pltpu.VMEM(block, F32),
                pltpu.VMEM(block, BF16), pltpu.VMEM(block, BF16),
                pltpu.VMEM((SPAN + 1, rows, rows), F32),
                pltpu.VMEM((nctx, per, width), BF16), pltpu.VMEM((nctx, per, width), BF16),
                pltpu.VMEM((nctx, per, width), BF16), pltpu.VMEM((nctx, per, width), BF16),
                pltpu.VMEM((heads, 1, width), F32), pltpu.VMEM((nctx, 1, width), F32),
                pltpu.VMEM((1, rows), F32), pltpu.VMEM((ntp, 1, rows), F32),
                dma((6,)), dma, dma, dma, dma, dma, dma, dma, dma,
            ] + [dma((2 * heads,))] * 8 + [dma((heads + 1,)), pltpu.SemaphoreType.REGULAR],
            compiler_params=pltpu.CompilerParams(
                collective_id=0, has_side_effects=True, vmem_limit_bytes=60 << 20),
            cost_estimate=pl.CostEstimate(flops=900_000_000, bytes_accessed=4 << 20, transcendentals=2_000_000),
        )(ql, kl, vl, dec, gain, qs, ks, vs, doc)
        return both[0], both[1]

    wide = P("tp", "ctx", None)
    return jax.shard_map(
        local, mesh=mesh,
        in_specs=(wide, wide, wide, P("tp", "ctx"), P("tp", None), wide, wide, wide, P()),
        out_specs=(wide, wide), check_vma=False)
```
